32 devices in a mesh: dp: 4 (over y, core), mp: 8 (over z, x).
Axes of the slice: x: 2, y: 2, z: 4, core: 2. Of those that a mesh axis runs over, the one named last changes fastest.
Arguments:
- prediction_maps: bfloat16 [4, 72, 384, 768], P('dp', None, 'mp'), may hold values from -6 to 6
- observed_maps: bfloat16 [4, 72, 384, 768], P('dp', None, 'mp'), may hold values from -6 to 6
- zonal_wavenumber_map: int32 [384], P('mp'), may hold values from 0 to 383, as said below
- associated_function_table: bfloat16 [384, 384, 384], P('mp', 'dp'), as said below
- magnitude_factor: float32 [384, 72], replicated, may hold values from 1 to 10
- phase_match_factor: float32 [384, 72], replicated, may hold values from 0.1 to 1
Outputs:
- grad_forecast: bfloat16 [4, 72, 384, 768], P('dp', None, 'mp')
The draws below stay inside these ranges and needn't reach their ends.
Inputs may be any that keep to these rules, and one draw needn't show every extreme that they name: `zonal_wavenumber_map`: slots stand 48 to an index of mp in order; each order appears in exactly one slot; in every index's block the first half holds orders below 192 and the second half orders of 192 or more. associated_function_table[s, q, l] is zero wherever l is below zonal_wavenumber_map[s].
All inputs are finite; a program needn't handle non-finite values.
Results may differ from the reference program's by a relative error of at most 0.008.
Values may be sent and summed in bfloat16 or wider, within the bound.
A program may use at most 192 MiB of HBM per device.

```python
import math
import jax
import jax.numpy as jnp
from jax import lax

OUTPUT_CHANNELS = 72
PARALLEL_CIRCLES = 384
MERIDIAN_POINTS = 768
HARMONIC_RANKS = 384
ORD_DEV = 48
SAMPLE_RUNS = 4


def slot_orders(key):
    groups = HARMONIC_RANKS // ORD_DEV
    half_slots = ORD_DEV // 2
    low_orders = jax.random.permutation(jax.random.fold_in(key, 11), HARMONIC_RANKS // 2).astype(jnp.int32)
    high_orders = jax.random.permutation(jax.random.fold_in(key, 12), HARMONIC_RANKS // 2).astype(jnp.int32) + HARMONIC_RANKS // 2
    blocks = jnp.concatenate([low_orders.reshape(groups, half_slots), high_orders.reshape(groups, half_slots)], axis=1)
    return blocks.reshape(HARMONIC_RANKS)


def draw_zonal_wavenumber_map(key, part):
    orders = slot_orders(key)
    return orders


def draw_associated_function_table(key, part):
    orders = slot_orders(key)
    key = jax.random.fold_in(key, 5)
    degree = jnp.arange(HARMONIC_RANKS, dtype=jnp.int32)
    nonzero = degree[None, None, :] >= orders[:, None, None]
    values = jax.random.normal(key, (HARMONIC_RANKS, PARALLEL_CIRCLES, HARMONIC_RANKS), jnp.float32)
    values = values / math.sqrt(PARALLEL_CIRCLES)
    return jnp.where(nonzero, values, 0.0).astype(jnp.bfloat16)


def levels(rng, shape, split, low, high):
    gain, own = 1.0, jax.random.fold_in(rng, 6)
    for position, shards_of in split:
        heights = jnp.exp(jax.random.uniform(jax.random.fold_in(own, position), (shards_of,), jnp.float32, low / len(split), high / len(split)))
        gain = gain * jnp.repeat(heights, shape[position] // shards_of).reshape([-1 if axis == position else 1 for axis in range(len(shape))])
    return gain


def scatter_about(key, extent, scale, bound, cuts=(), held_as=jnp.bfloat16):
    array = jax.random.normal(key, extent, jnp.float32) * scale
    if len(cuts) > 0:
        array = levels(key, extent, cuts, -0.22, 0.18) * array
    return jnp.clip(array, min=-bound, max=bound).astype(held_as)


def setup_inputs(seed: int = 0) -> dict:
    seeds = jax.random.split(jax.random.key(seed), 7)
    prediction_maps = scatter_about(seeds[0], (SAMPLE_RUNS, OUTPUT_CHANNELS, PARALLEL_CIRCLES, MERIDIAN_POINTS), 1.0, 6.0, ((0, 4), (2, 8)))
    observed_maps = scatter_about(seeds[1], (SAMPLE_RUNS, OUTPUT_CHANNELS, PARALLEL_CIRCLES, MERIDIAN_POINTS), 1.0, 6.0, ((0, 4), (2, 8)))
    zonal_wavenumber_map = draw_zonal_wavenumber_map(jax.random.fold_in(seeds[6], 71), 0)
    associated_function_table = draw_associated_function_table(jax.random.fold_in(seeds[6], 71), 0)
    magnitude_factor = jnp.clip(jnp.exp(jax.random.uniform(seeds[4], (HARMONIC_RANKS, OUTPUT_CHANNELS), jnp.float32, math.log(1.0), math.log(10.0))), 1.0, 10.0)
    phase_match_factor = jnp.clip(jnp.exp(jax.random.uniform(seeds[5], (HARMONIC_RANKS, OUTPUT_CHANNELS), jnp.float32, math.log(0.1), math.log(1.0))), 0.1, 1.0)
    return dict(prediction_maps=prediction_maps, observed_maps=observed_maps, zonal_wavenumber_map=zonal_wavenumber_map, associated_function_table=associated_function_table, magnitude_factor=magnitude_factor, phase_match_factor=phase_match_factor)


def transform_table(orders):
    longitude = jnp.arange(MERIDIAN_POINTS, dtype=jnp.int32)
    phase_index = longitude[:, None] * orders[None, :].astype(jnp.int32) % MERIDIAN_POINTS
    radians = phase_index.astype(jnp.float32) * (2.0 * math.pi / MERIDIAN_POINTS)
    norm_factor = 1.0 / math.sqrt(MERIDIAN_POINTS)
    return jnp.stack([jnp.cos(radians) * norm_factor, -jnp.sin(radians) * norm_factor], axis=1).astype(jnp.bfloat16)

def reference(prediction_maps, observed_maps, zonal_wavenumber_map, associated_function_table, magnitude_factor, phase_match_factor):
    fourier_f32 = transform_table(zonal_wavenumber_map).astype(jnp.float32)
    analysis = associated_function_table.astype(jnp.float32)
    order_weight = jnp.where(zonal_wavenumber_map == 0, 1.0, 2.0).astype(jnp.float32)

    def analyse(member_grid):
        mode_energies = jnp.einsum('cqo,okm->mqkc', member_grid.astype(jnp.float32), fourier_f32)
        mode_energies = mode_energies.reshape(HARMONIC_RANKS, PARALLEL_CIRCLES, 2 * OUTPUT_CHANNELS).astype(jnp.bfloat16)
        return jnp.einsum('sql,sqk->slk', analysis, mode_energies.astype(jnp.float32))

    def order_power(harmonic_expansion):
        quadratic_terms = harmonic_expansion[..., :OUTPUT_CHANNELS] ** 2 + harmonic_expansion[..., OUTPUT_CHANNELS:] ** 2
        return lax.optimization_barrier(jnp.sum(order_weight[:, None, None] * quadratic_terms, axis=0)) + 1.0

    def sample_position(member_grids):
        coef_pred = analyse(member_grids[0])
        coef_true = analyse(member_grids[1])
        power_ratio = jnp.sqrt(order_power(coef_true) / order_power(coef_pred))
        pred_factor = 2.0 * magnitude_factor * (1.0 - power_ratio) + 2.0 * phase_match_factor * power_ratio
        true_factor = -2.0 * phase_match_factor
        pred_wide = jnp.concatenate([pred_factor, pred_factor], axis=1)
        true_wide = jnp.concatenate([true_factor, true_factor], axis=1)
        grad_coef = (order_weight[:, None, None] * (pred_wide * coef_pred + true_wide * coef_true)).astype(jnp.bfloat16)
        spectral_sensitivity = jnp.einsum('sql,slk->sqk', analysis, grad_coef.astype(jnp.float32)).astype(jnp.bfloat16)
        spectral_sensitivity = spectral_sensitivity.reshape(HARMONIC_RANKS, PARALLEL_CIRCLES, 2, OUTPUT_CHANNELS).astype(jnp.float32)
        grad_grid = jnp.einsum('okm,mqkc->cqo', fourier_f32, spectral_sensitivity)
        return grad_grid.astype(jnp.bfloat16)
    return lax.map(sample_position, (prediction_maps, observed_maps))
```

```python
import math

import jax
import jax.numpy as jnp
from jax import lax
from jax.sharding import PartitionSpec as P

MERIDIAN_POINTS = 768
GROUPS = 3


def transform_table(orders, blocks):
    longitude = jnp.arange(MERIDIAN_POINTS, dtype=jnp.int32)
    phase_index = longitude[:, None] * orders[None, :] % MERIDIAN_POINTS
    radians = phase_index.astype(jnp.float32) * (2.0 * math.pi / MERIDIAN_POINTS)
    norm_factor = 1.0 / math.sqrt(MERIDIAN_POINTS)
    cosine = (jnp.cos(radians) * norm_factor).astype(jnp.bfloat16)
    sine = (-jnp.sin(radians) * norm_factor).astype(jnp.bfloat16)
    slots = orders.shape[0] // blocks
    both = jnp.stack(
        [
            cosine.reshape(MERIDIAN_POINTS, blocks, slots),
            sine.reshape(MERIDIAN_POINTS, blocks, slots),
        ],
        axis=2,
    )
    return both.reshape(MERIDIAN_POINTS, 2 * orders.shape[0])


def local(
    blocks,
    prediction_maps,
    observed_maps,
    zonal_wavenumber_map,
    associated_function_table,
    magnitude_factor,
    phase_match_factor,
):
    orders = lax.all_gather(zonal_wavenumber_map, "mp", axis=0, tiled=True)
    fourier = transform_table(orders, blocks)
    full_table = lax.all_gather(associated_function_table, "dp", axis=1, tiled=True)
    channels, lat_dev = prediction_maps.shape[1:3]
    slots, latitudes, degrees = full_table.shape
    part = channels // GROUPS
    order_weight = jnp.where(zonal_wavenumber_map == 0, 1.0, 2.0).astype(jnp.float32)
    magnitude, phase = magnitude_factor.T, phase_match_factor.T

    def to_slots(fields):
        grid = fields.reshape(part * lat_dev, MERIDIAN_POINTS)
        spec = lax.dot_general(
            fourier, grid, (((0,), (1,)), ((), ())), preferred_element_type=jnp.float32
        ).astype(jnp.bfloat16)
        spec = spec.reshape(blocks, 2 * slots, part * lat_dev)
        spec = lax.all_to_all(spec, "mp", split_axis=0, concat_axis=0, tiled=True)
        spec = spec.reshape(blocks, 2, slots, part, lat_dev)
        return spec.transpose(2, 1, 3, 0, 4).reshape(slots, 2 * part, latitudes)

    def analyse(spec):
        return jnp.einsum(
            "sjq,sql->sjl", spec, full_table, preferred_element_type=jnp.float32
        ).reshape(slots, 2, part, degrees)

    def order_power(coef):
        return jnp.sum(order_weight[:, None, None, None] * coef * coef, axis=(0, 1))

    results = []
    for group in range(GROUPS):
        rows = slice(group * part, (group + 1) * part)
        coef_pred = analyse(to_slots(prediction_maps[0, rows]))
        coef_true = analyse(to_slots(observed_maps[0, rows]))
        partial = jnp.stack([order_power(coef_pred), order_power(coef_true)])
        if group > 0:
            partial, _ = lax.optimization_barrier((partial, power))
        power = lax.psum(partial, "mp") + 1.0
        ratio = jnp.sqrt(power[1] / power[0])
        pred_factor = 2.0 * magnitude[rows] * (1.0 - ratio) + 2.0 * phase[rows] * ratio
        true_factor = -2.0 * phase[rows]
        grad_coef = (
            order_weight[:, None, None, None] * (pred_factor * coef_pred + true_factor * coef_true)
        ).astype(jnp.bfloat16)
        grad_spec = jnp.einsum(
            "sjl,sql->sjq",
            grad_coef.reshape(slots, 2 * part, degrees),
            full_table,
            preferred_element_type=jnp.float32,
        ).astype(jnp.bfloat16)
        grad_spec = grad_spec.reshape(slots, 2, part, blocks, lat_dev).transpose(3, 1, 0, 2, 4)
        grad_spec = grad_spec.reshape(blocks, 2 * slots, part * lat_dev)
        grad_lat = lax.all_to_all(grad_spec, "mp", split_axis=0, concat_axis=0, tiled=True)
        grad_grid = lax.dot_general(
            grad_lat.reshape(2 * blocks * slots, part * lat_dev),
            fourier,
            (((0,), (1,)), ((), ())),
            preferred_element_type=jnp.float32,
        ).astype(jnp.bfloat16)
        results.append(grad_grid.reshape(part, lat_dev, MERIDIAN_POINTS))
    return jnp.concatenate(results, axis=0)[None]


def solution(mesh):
    blocks = mesh.shape["mp"]

    def run(*arrays):
        return local(blocks, *arrays)

    return jax.shard_map(
        run,
        mesh=mesh,
        in_specs=(
            P("dp", None, "mp", None),
            P("dp", None, "mp", None),
            P("mp"),
            P("mp", "dp", None),
            P(),
            P(),
        ),
        out_specs=P("dp", None, "mp", None),
        check_vma=False,
    )
```

```python
import math

import jax
import jax.numpy as jnp
from jax import lax
from jax.sharding import PartitionSpec as P

MERIDIAN_POINTS = 768
CUTS = (0, 3, 6, 8, 9)


def transform_table(orders, blocks):
    longitude = jnp.arange(MERIDIAN_POINTS, dtype=jnp.int32)
    phase_index = longitude[:, None] * orders[None, :] % MERIDIAN_POINTS
    radians = phase_index.astype(jnp.float32) * (2.0 * math.pi / MERIDIAN_POINTS)
    norm_factor = 1.0 / math.sqrt(MERIDIAN_POINTS)
    cosine = (jnp.cos(radians) * norm_factor).astype(jnp.bfloat16)
    sine = (-jnp.sin(radians) * norm_factor).astype(jnp.bfloat16)
    slots = orders.shape[0] // blocks
    both = jnp.stack(
        [
            cosine.reshape(MERIDIAN_POINTS, blocks, slots),
            sine.reshape(MERIDIAN_POINTS, blocks, slots),
        ],
        axis=2,
    )
    return both.reshape(MERIDIAN_POINTS, 2 * orders.shape[0])


def local(
    blocks,
    prediction_maps,
    observed_maps,
    zonal_wavenumber_map,
    associated_function_table,
    magnitude_factor,
    phase_match_factor,
):
    last = [zonal_wavenumber_map]

    def exchange(array):
        array, _ = lax.optimization_barrier((array, last[0]))
        last[0] = lax.all_to_all(array, "mp", split_axis=0, concat_axis=0, tiled=True)
        return last[0]

    def share(array):
        return exchange(jnp.broadcast_to(array[None], (blocks,) + array.shape))

    channels, lat_dev = prediction_maps.shape[1:3]
    slots = zonal_wavenumber_map.shape[0]
    full_table = lax.all_gather(associated_function_table, "dp", axis=1, tiled=True)
    latitudes, degrees = full_table.shape[1:]
    orders = share(zonal_wavenumber_map[None]).reshape(blocks * slots)
    fourier = transform_table(orders, blocks)
    order_weight = jnp.where(zonal_wavenumber_map == 0, 1.0, 2.0).astype(jnp.float32)
    magnitude, phase = magnitude_factor.T, phase_match_factor.T

    def to_slots(rows):
        part = rows.stop - rows.start
        grid = jnp.concatenate([prediction_maps[0, rows], observed_maps[0, rows]], axis=0)
        spec = lax.dot_general(
            fourier,
            grid.reshape(2 * part * lat_dev, MERIDIAN_POINTS),
            (((0,), (1,)), ((), ())),
            preferred_element_type=jnp.float32,
        ).astype(jnp.bfloat16)
        return exchange(spec.reshape(blocks, 2 * slots, 2 * part * lat_dev))

    def analyse(spec, rows):
        part = rows.stop - rows.start
        spec = spec.reshape(blocks, 2, slots, 2 * part, lat_dev)
        spec = spec.transpose(2, 1, 3, 0, 4).reshape(slots, 4 * part, latitudes)
        coef = jnp.einsum("sjq,sql->sjl", spec, full_table, preferred_element_type=jnp.float32)
        coef = coef.reshape(slots, 2, 2, part, degrees)
        return coef, jnp.sum(order_weight[:, None, None, None, None] * coef * coef, axis=(0, 1))

    def sum_orders(power):
        width = math.gcd(128, power.size // blocks)
        pieces = exchange(power.reshape(blocks, power.size // (blocks * width), width))
        return share(jnp.sum(pieces, axis=0)).reshape(power.shape) + 1.0

    def synthesise(coef, power, rows):
        part = rows.stop - rows.start
        ratio = jnp.sqrt(power[1] / power[0])
        pred_factor = 2.0 * magnitude[rows] * (1.0 - ratio) + 2.0 * phase[rows] * ratio
        true_factor = -2.0 * phase[rows]
        grad_coef = (
            order_weight[:, None, None, None]
            * (pred_factor * coef[:, :, 0] + true_factor * coef[:, :, 1])
        ).astype(jnp.bfloat16)
        grad_spec = jnp.einsum(
            "sjl,sql->sjq",
            grad_coef.reshape(slots, 2 * part, degrees),
            full_table,
            preferred_element_type=jnp.float32,
        ).astype(jnp.bfloat16)
        grad_spec = grad_spec.reshape(slots, 2, part, blocks, lat_dev).transpose(3, 1, 0, 2, 4)
        return grad_spec.reshape(blocks, 2 * slots, part * lat_dev)

    def to_grid(grad_spec, rows):
        part = rows.stop - rows.start
        grad_grid = lax.dot_general(
            exchange(grad_spec).reshape(2 * blocks * slots, part * lat_dev),
            fourier,
            (((0,), (1,)), ((), ())),
            preferred_element_type=jnp.float32,
        ).astype(jnp.bfloat16)
        return grad_grid.reshape(part, lat_dev, MERIDIAN_POINTS)

    bounds = [channels * cut // 9 for cut in CUTS]
    groups = [slice(low, high) for low, high in zip(bounds[:-1], bounds[1:])]
    count = len(groups)
    spec, coef, power, grad, results = {}, {}, {}, {}, {}

    def forward(group):
        spec[group] = to_slots(groups[group])

    def legendre(group):
        coef[group], partial = analyse(spec[group], groups[group])
        power[group] = sum_orders(partial)
        grad[group] = synthesise(coef[group], power[group], groups[group])

    def backward(group):
        results[group] = to_grid(grad[group], groups[group])

    forward(0)
    for group in range(1, count):
        forward(group)
        legendre(group - 1)
    for group in range(count - 2):
        backward(group)
    legendre(count - 1)
    backward(count - 2)
    backward(count - 1)
    return jnp.concatenate([results[group] for group in range(count)], axis=0)[None]


def solution(mesh):
    blocks = mesh.shape["mp"]

    def run(*arrays):
        return local(blocks, *arrays)

    return jax.shard_map(
        run,
        mesh=mesh,
        in_specs=(
            P("dp", None, "mp", None),
            P("dp", None, "mp", None),
            P("mp"),
            P("mp", "dp", None),
            P(),
            P(),
        ),
        out_specs=P("dp", None, "mp", None),
        check_vma=False,
    )
```

```python
import math

import jax
import jax.numpy as jnp
from jax import lax
from jax.sharding import PartitionSpec as P

MERIDIAN_POINTS = 768


def transform_table(orders):
    longitude = jnp.arange(MERIDIAN_POINTS, dtype=jnp.int32)
    phase_index = longitude[:, None] * orders[None, :] % MERIDIAN_POINTS
    radians = phase_index.astype(jnp.float32) * (2.0 * math.pi / MERIDIAN_POINTS)
    norm_factor = 1.0 / math.sqrt(MERIDIAN_POINTS)
    return jnp.stack(
        [jnp.cos(radians) * norm_factor, -jnp.sin(radians) * norm_factor], axis=1
    ).astype(jnp.bfloat16)


def local(
    blocks,
    prediction_maps,
    observed_maps,
    zonal_wavenumber_map,
    associated_function_table,
    magnitude_factor,
    phase_match_factor,
):
    last = [zonal_wavenumber_map]

    def exchange(array):
        array, _ = lax.optimization_barrier((array, last[0]))
        last[0] = lax.all_to_all(array, "mp", split_axis=0, concat_axis=0, tiled=True)
        return last[0]

    def share(array):
        return exchange(jnp.broadcast_to(array[None], (blocks,) + array.shape))

    channels, lat_dev = prediction_maps.shape[1:3]
    slots = zonal_wavenumber_map.shape[0]
    full_table = lax.all_gather(associated_function_table, "dp", axis=1, tiled=True)
    latitudes, degrees = full_table.shape[1:]
    orders = share(zonal_wavenumber_map[None]).reshape(blocks * slots)
    by_part = transform_table(orders)
    fourier = by_part.reshape(MERIDIAN_POINTS, 2, blocks, slots).transpose(0, 2, 1, 3)
    fourier = fourier.reshape(MERIDIAN_POINTS, 2 * blocks * slots)
    order_weight = jnp.where(zonal_wavenumber_map == 0, 1.0, 2.0).astype(jnp.float32)
    magnitude, phase = magnitude_factor.T, phase_match_factor.T

    def to_slots(rows):
        part = rows.stop - rows.start
        grid = jnp.concatenate([prediction_maps[0, rows], observed_maps[0, rows]], axis=0)
        spec = lax.dot_general(
            fourier,
            grid.reshape(2 * part * lat_dev, MERIDIAN_POINTS),
            (((0,), (1,)), ((), ())),
            preferred_element_type=jnp.float32,
        ).astype(jnp.bfloat16)
        return spec.reshape(blocks, 2 * slots, 2 * part * lat_dev)

    def to_slots_wide(rows):
        part = rows.stop - rows.start
        both = [
            jnp.einsum(
                "cqn,nkm->mqkc", fields[0, rows], by_part, preferred_element_type=jnp.float32
            ).astype(jnp.bfloat16)
            for fields in (prediction_maps, observed_maps)
        ]
        spec = jnp.stack(both, axis=2)
        return spec.reshape(blocks, slots, lat_dev, 4 * part)

    def narrow_lines(spec, rows):
        part = rows.stop - rows.start
        spec = spec.reshape(blocks, 2, slots, 2, part, lat_dev)
        return spec.transpose(2, 3, 1, 4, 0, 5).reshape(slots, 4 * part, latitudes)

    def analyse(coef, rows):
        part = rows.stop - rows.start
        coef = coef.reshape(slots, 2, 2, part, degrees)
        return coef, jnp.sum(order_weight[:, None, None, None, None] * coef * coef, axis=(0, 2))

    def sum_orders(power):
        width = math.gcd(128, power.size // blocks)
        pieces = exchange(power.reshape(blocks, power.size // (blocks * width), width))
        return share(jnp.sum(pieces, axis=0)).reshape(power.shape) + 1.0

    def synthesise(coef, power, rows):
        part = rows.stop - rows.start
        ratio = jnp.sqrt(power[1] / power[0])
        pred_factor = 2.0 * magnitude[rows] * (1.0 - ratio) + 2.0 * phase[rows] * ratio
        true_factor = -2.0 * phase[rows]
        grad_coef = (
            order_weight[:, None, None, None]
            * (pred_factor * coef[:, 0] + true_factor * coef[:, 1])
        ).astype(jnp.bfloat16)
        grad_spec = jnp.einsum(
            "sjl,sql->sjq",
            grad_coef.reshape(slots, 2 * part, degrees),
            full_table,
            preferred_element_type=jnp.float32,
        ).astype(jnp.bfloat16)
        grad_spec = grad_spec.reshape(slots, 2, part, blocks, lat_dev).transpose(3, 1, 0, 2, 4)
        return grad_spec.reshape(blocks, 2 * slots, part * lat_dev)

    def to_grid(grad_spec, rows):
        part = rows.stop - rows.start
        grad_grid = lax.dot_general(
            exchange(grad_spec).reshape(2 * blocks * slots, part * lat_dev),
            fourier,
            (((0,), (1,)), ((), ())),
            preferred_element_type=jnp.float32,
        ).astype(jnp.bfloat16)
        return grad_grid.reshape(part, lat_dev, MERIDIAN_POINTS)

    narrow = channels // 9
    middle = (channels + narrow) // 2
    groups = [slice(0, narrow), slice(narrow, middle), slice(middle, channels)]

    def after(array):
        return lax.optimization_barrier((array, last[0]))[0]

    def legendre_narrow(spec):
        return jnp.einsum(
            "sjq,sql->sjl",
            narrow_lines(spec, groups[0]),
            full_table,
            preferred_element_type=jnp.float32,
        )

    def legendre_wide(spec, table):
        lines = spec.transpose(1, 0, 2, 3).reshape(table.shape[0], latitudes, spec.shape[3])
        return jnp.einsum("sqj,sql->sjl", lines, table, preferred_element_type=jnp.float32)

    half = slots // 2
    spec_0 = exchange(to_slots(groups[0]))
    spec_1 = exchange(to_slots_wide(groups[1]))
    coef_0, partial_0 = analyse(legendre_narrow(spec_0), groups[0])
    payload_2 = to_slots_wide(groups[2])
    power_0 = sum_orders(partial_0)
    spec_1 = after(spec_1)
    low_2 = exchange(payload_2[:, :half])
    coef_1, partial_1 = analyse(legendre_wide(spec_1, full_table), groups[1])
    power_1 = sum_orders(partial_1)
    coef_0, coef_1 = after((coef_0, coef_1))
    high_2 = exchange(payload_2[:, half:])
    grad_0 = synthesise(coef_0, power_0, groups[0])
    grad_1 = synthesise(coef_1, power_1, groups[1])
    result_0 = to_grid(grad_0, groups[0])
    spec_2 = jnp.concatenate([low_2, high_2], axis=1)
    coef_2, partial_2 = analyse(legendre_wide(spec_2, full_table), groups[2])
    power_2 = sum_orders(partial_2)
    coef_2 = after(coef_2)
    result_1 = to_grid(grad_1, groups[1])
    result_2 = to_grid(synthesise(coef_2, power_2, groups[2]), groups[2])
    return jnp.concatenate([result_0, result_1, result_2], axis=0)[None]


def solution(mesh):
    blocks = mesh.shape["mp"]

    def run(*arrays):
        return local(blocks, *arrays)

    return jax.shard_map(
        run,
        mesh=mesh,
        in_specs=(
            P("dp", None, "mp", None),
            P("dp", None, "mp", None),
            P("mp"),
            P("mp", "dp", None),
            P(),
            P(),
        ),
        out_specs=P("dp", None, "mp", None),
        check_vma=False,
    )
```

```python
import math

import jax
import jax.numpy as jnp
from jax import lax
from jax.experimental.layout import Layout, with_layout_constraint
from jax.sharding import PartitionSpec as P

MERIDIAN_POINTS = 768


def transform_table(orders):
    longitude = jnp.arange(MERIDIAN_POINTS, dtype=jnp.int32)
    phase_index = longitude[:, None] * orders[None, :] % MERIDIAN_POINTS
    radians = phase_index.astype(jnp.float32) * (2.0 * math.pi / MERIDIAN_POINTS)
    norm_factor = 1.0 / math.sqrt(MERIDIAN_POINTS)
    return jnp.stack(
        [jnp.cos(radians) * norm_factor, -jnp.sin(radians) * norm_factor], axis=1
    ).astype(jnp.bfloat16)


def local(
    blocks,
    prediction_maps,
    observed_maps,
    zonal_wavenumber_map,
    associated_function_table,
    magnitude_factor,
    phase_match_factor,
):
    last = [zonal_wavenumber_map]

    def exchange(array):
        array, _ = lax.optimization_barrier((array, last[0]))
        last[0] = lax.all_to_all(array, "mp", split_axis=0, concat_axis=0, tiled=True)
        return last[0]

    def share(array):
        return exchange(jnp.broadcast_to(array[None], (blocks,) + array.shape))

    channels, lat_dev = prediction_maps.shape[1:3]
    slots = zonal_wavenumber_map.shape[0]
    full_table = lax.all_gather(associated_function_table, "dp", axis=1, tiled=True)
    latitudes, degrees = full_table.shape[1:]
    orders = share(zonal_wavenumber_map[None]).reshape(blocks * slots)
    by_part = transform_table(orders)
    fourier = by_part.reshape(MERIDIAN_POINTS, 2, blocks, slots).transpose(0, 2, 1, 3)
    fourier = fourier.reshape(MERIDIAN_POINTS, 2 * blocks * slots)
    order_weight = jnp.where(zonal_wavenumber_map == 0, 1.0, 2.0).astype(jnp.float32)
    magnitude, phase = magnitude_factor.T, phase_match_factor.T

    def to_slots(rows):
        part = rows.stop - rows.start
        grid = jnp.concatenate([prediction_maps[0, rows], observed_maps[0, rows]], axis=0)
        spec = lax.dot_general(
            fourier,
            grid.reshape(2 * part * lat_dev, MERIDIAN_POINTS),
            (((0,), (1,)), ((), ())),
            preferred_element_type=jnp.float32,
        ).astype(jnp.bfloat16)
        return spec.reshape(blocks, 2 * slots, 2 * part * lat_dev)

    def to_slots_wide(rows, table):
        part = rows.stop - rows.start
        both = [
            jnp.einsum(
                "cqn,nkm->mqkc", fields[0, rows], table, preferred_element_type=jnp.float32
            ).astype(jnp.bfloat16)
            for fields in (prediction_maps, observed_maps)
        ]
        spec = jnp.stack(both, axis=2)
        spec = spec.reshape(blocks, spec.shape[0] // blocks, lat_dev, 4 * part)
        return with_layout_constraint(spec, Layout(major_to_minor=(0, 1, 2, 3)))

    def narrow_lines(spec, rows):
        part = rows.stop - rows.start
        spec = spec.reshape(blocks, 2, slots, 2, part, lat_dev)
        return spec.transpose(2, 3, 1, 4, 0, 5).reshape(slots, 4 * part, latitudes)

    def analyse(coef, rows):
        part = rows.stop - rows.start
        coef = coef.reshape(slots, 2, 2, part, degrees)
        return coef, jnp.sum(order_weight[:, None, None, None, None] * coef * coef, axis=(0, 2))

    def sum_orders(power):
        width = math.gcd(128, power.size // blocks)
        pieces = exchange(power.reshape(blocks, power.size // (blocks * width), width))
        return share(jnp.sum(pieces, axis=0)).reshape(power.shape) + 1.0

    def synthesise(coef, power, rows):
        part = rows.stop - rows.start
        ratio = jnp.sqrt(power[1] / power[0])
        pred_factor = 2.0 * magnitude[rows] * (1.0 - ratio) + 2.0 * phase[rows] * ratio
        true_factor = -2.0 * phase[rows]
        grad_coef = (
            order_weight[:, None, None, None]
            * (pred_factor * coef[:, 0] + true_factor * coef[:, 1])
        ).astype(jnp.bfloat16)
        grad_spec = jnp.einsum(
            "sjl,sql->sjq",
            grad_coef.reshape(slots, 2 * part, degrees),
            full_table,
            preferred_element_type=jnp.float32,
        ).astype(jnp.bfloat16)
        grad_spec = grad_spec.reshape(slots, 2, part, blocks, lat_dev).transpose(3, 1, 0, 2, 4)
        return grad_spec.reshape(blocks, 2 * slots, part * lat_dev)

    def to_grid(grad_lat, rows):
        part = rows.stop - rows.start
        grad_grid = lax.dot_general(
            grad_lat.reshape(2 * blocks * slots, part * lat_dev),
            fourier,
            (((0,), (1,)), ((), ())),
            preferred_element_type=jnp.float32,
        ).astype(jnp.bfloat16)
        return grad_grid.reshape(part, lat_dev, MERIDIAN_POINTS)

    narrow = channels // 9
    middle = (channels + narrow) // 2
    groups = [slice(0, narrow), slice(narrow, middle), slice(middle, channels)]

    def after(array):
        return lax.optimization_barrier((array, last[0]))[0]

    def legendre_narrow(spec):
        return jnp.einsum(
            "sjq,sql->sjl",
            narrow_lines(spec, groups[0]),
            full_table,
            preferred_element_type=jnp.float32,
        )

    def legendre_wide(spec, table):
        lines = spec.transpose(1, 0, 2, 3).reshape(table.shape[0], latitudes, spec.shape[3])
        return jnp.einsum("sqj,sql->sjl", lines, table, preferred_element_type=jnp.float32)

    half = slots // 2
    by_half = by_part.reshape(MERIDIAN_POINTS, 2, blocks, 2, half)
    spec_0 = exchange(to_slots(groups[0]))
    by_half = after(by_half)
    low_table, high_table = (
        by_half[:, :, :, side].reshape(MERIDIAN_POINTS, 2, blocks * half) for side in (0, 1)
    )
    spec_1 = exchange(to_slots_wide(groups[1], by_part))
    coef_0, partial_0 = analyse(legendre_narrow(spec_0), groups[0])
    low_2 = to_slots_wide(groups[2], low_table)
    high_2 = to_slots_wide(groups[2], high_table)
    partial_0, low_2, high_2 = lax.optimization_barrier((partial_0, low_2, high_2))
    power_0 = sum_orders(partial_0)
    spec_1 = after(spec_1)
    low_2 = exchange(low_2)
    coef_1, partial_1 = analyse(legendre_wide(spec_1, full_table), groups[1])
    grad_0 = synthesise(coef_0, power_0, groups[0])
    partial_1, grad_0 = lax.optimization_barrier((partial_1, grad_0))
    power_1 = sum_orders(partial_1)
    high_2 = exchange(high_2)
    grad_1 = synthesise(coef_1, power_1, groups[1])
    grad_cosine, grad_sine = lax.optimization_barrier((grad_1[:, :slots], grad_1[:, slots:]))
    cosine_1 = exchange(grad_cosine)
    spec_2 = jnp.concatenate([low_2, high_2], axis=1)
    coef_2, partial_2 = analyse(legendre_wide(spec_2, full_table), groups[2])
    power_2 = sum_orders(partial_2)
    sine_1 = exchange(grad_sine)
    grad_2 = synthesise(coef_2, power_2, groups[2])
    lat_0 = exchange(grad_0)
    lat_2 = exchange(grad_2)
    results = [
        to_grid(lat_0, groups[0]),
        to_grid(jnp.concatenate([cosine_1, sine_1], axis=1), groups[1]),
        to_grid(lat_2, groups[2]),
    ]
    return jnp.concatenate(results, axis=0)[None]


def solution(mesh):
    blocks = mesh.shape["mp"]

    def run(*arrays):
        return local(blocks, *arrays)

    return jax.shard_map(
        run,
        mesh=mesh,
        in_specs=(
            P("dp", None, "mp", None),
            P("dp", None, "mp", None),
            P("mp"),
            P("mp", "dp", None),
            P(),
            P(),
        ),
        out_specs=P("dp", None, "mp", None),
        check_vma=False,
    )
```

```python
import math

import jax
import jax.numpy as jnp
from jax import lax
from jax.experimental.layout import Layout, with_layout_constraint
from jax.sharding import PartitionSpec as P

MERIDIAN_POINTS = 768


def transform_table(orders):
    longitude = jnp.arange(MERIDIAN_POINTS, dtype=jnp.int32)
    phase_index = longitude[:, None] * orders[None, :] % MERIDIAN_POINTS
    radians = phase_index.astype(jnp.float32) * (2.0 * math.pi / MERIDIAN_POINTS)
    norm_factor = 1.0 / math.sqrt(MERIDIAN_POINTS)
    return jnp.stack(
        [jnp.cos(radians) * norm_factor, -jnp.sin(radians) * norm_factor], axis=1
    ).astype(jnp.bfloat16)


def local(
    blocks,
    prediction_maps,
    observed_maps,
    zonal_wavenumber_map,
    associated_function_table,
    magnitude_factor,
    phase_match_factor,
):
    last = [zonal_wavenumber_map]

    def exchange(array):
        array, _ = lax.optimization_barrier((array, last[0]))
        last[0] = lax.all_to_all(array, "mp", split_axis=0, concat_axis=0, tiled=True)
        return last[0]

    def share(array):
        return exchange(jnp.broadcast_to(array[None], (blocks,) + array.shape))

    channels, lat_dev = prediction_maps.shape[1:3]
    slots = zonal_wavenumber_map.shape[0]
    full_table = lax.all_gather(associated_function_table, "dp", axis=1, tiled=True)
    latitudes, degrees = full_table.shape[1:]
    orders = share(zonal_wavenumber_map[None]).reshape(blocks * slots)
    by_part = transform_table(orders)
    fourier = by_part.reshape(MERIDIAN_POINTS, 2, blocks, slots).transpose(0, 2, 1, 3)
    fourier = fourier.reshape(MERIDIAN_POINTS, 2 * blocks * slots)
    order_weight = jnp.where(zonal_wavenumber_map == 0, 1.0, 2.0).astype(jnp.float32)
    magnitude, phase = magnitude_factor.T, phase_match_factor.T

    def to_slots(rows):
        part = rows.stop - rows.start
        grid = jnp.concatenate([prediction_maps[0, rows], observed_maps[0, rows]], axis=0)
        spec = lax.dot_general(
            fourier,
            grid.reshape(2 * part * lat_dev, MERIDIAN_POINTS),
            (((0,), (1,)), ((), ())),
            preferred_element_type=jnp.float32,
        ).astype(jnp.bfloat16)
        return spec.reshape(blocks, 2 * slots, 2 * part * lat_dev)

    def to_slots_wide(rows, table):
        part = rows.stop - rows.start
        both = [
            jnp.einsum(
                "cqn,nkm->mqkc", fields[0, rows], table, preferred_element_type=jnp.float32
            ).astype(jnp.bfloat16)
            for fields in (prediction_maps, observed_maps)
        ]
        spec = jnp.stack(both, axis=2)
        spec = spec.reshape(blocks, spec.shape[0] // blocks, lat_dev, 4 * part)
        return with_layout_constraint(spec, Layout(major_to_minor=(0, 1, 2, 3)))

    def narrow_lines(spec, rows):
        part = rows.stop - rows.start
        spec = spec.reshape(blocks, 2, slots, 2, part, lat_dev)
        return spec.transpose(2, 3, 1, 4, 0, 5).reshape(slots, 4 * part, latitudes)

    def analyse(coef, rows):
        part = rows.stop - rows.start
        coef = coef.reshape(slots, 2, 2, part, degrees)
        return coef, jnp.sum(order_weight[:, None, None, None, None] * coef * coef, axis=(0, 2))

    def sum_orders(power):
        width = math.gcd(128, power.size // blocks)
        pieces = exchange(power.reshape(blocks, power.size // (blocks * width), width))
        return share(jnp.sum(pieces, axis=0)).reshape(power.shape) + 1.0

    def synthesise(coef, power, rows):
        part = rows.stop - rows.start
        ratio = jnp.sqrt(power[1] / power[0])
        pred_factor = 2.0 * magnitude[rows] * (1.0 - ratio) + 2.0 * phase[rows] * ratio
        true_factor = -2.0 * phase[rows]
        grad_coef = (
            order_weight[:, None, None, None]
            * (pred_factor * coef[:, 0] + true_factor * coef[:, 1])
        ).astype(jnp.bfloat16)
        grad_spec = jnp.einsum(
            "sjl,sql->sjq",
            grad_coef.reshape(slots, 2 * part, degrees),
            full_table,
            preferred_element_type=jnp.float32,
        ).astype(jnp.bfloat16)
        grad_spec = grad_spec.reshape(slots, 2, part, blocks, lat_dev).transpose(3, 1, 0, 2, 4)
        return grad_spec.reshape(blocks, 2 * slots, part * lat_dev)

    def to_grid(grad_lat, rows):
        part = rows.stop - rows.start
        grad_grid = lax.dot_general(
            grad_lat.reshape(2 * blocks * slots, part * lat_dev),
            fourier,
            (((0,), (1,)), ((), ())),
            preferred_element_type=jnp.float32,
        ).astype(jnp.bfloat16)
        return grad_grid.reshape(part, lat_dev, MERIDIAN_POINTS)

    narrow = channels // 9
    middle = (channels + narrow) // 2
    groups = [slice(0, narrow), slice(narrow, middle), slice(middle, channels)]

    def after(array):
        return lax.optimization_barrier((array, last[0]))[0]

    def legendre_narrow(spec):
        return jnp.einsum(
            "sjq,sql->sjl",
            narrow_lines(spec, groups[0]),
            full_table,
            preferred_element_type=jnp.float32,
        )

    def legendre_wide(spec, table):
        lines = spec.transpose(1, 0, 2, 3).reshape(table.shape[0], latitudes, spec.shape[3])
        return jnp.einsum("sqj,sql->sjl", lines, table, preferred_element_type=jnp.float32)

    half = slots // 2
    by_half = by_part.reshape(MERIDIAN_POINTS, 2, blocks, 2, half)
    spec_0 = exchange(to_slots(groups[0]))
    by_half = after(by_half)
    low_table, high_table = (
        by_half[:, :, :, side].reshape(MERIDIAN_POINTS, 2, blocks * half) for side in (0, 1)
    )
    spec_1 = exchange(to_slots_wide(groups[1], by_part))
    coef_0, partial_0 = analyse(legendre_narrow(spec_0), groups[0])
    low_2 = to_slots_wide(groups[2], low_table)
    high_2 = to_slots_wide(groups[2], high_table)
    partial_0, low_2, high_2 = lax.optimization_barrier((partial_0, low_2, high_2))
    power_0 = sum_orders(partial_0)
    spec_1 = after(spec_1)
    low_2 = exchange(low_2)
    coef_1, partial_1 = analyse(legendre_wide(spec_1, full_table), groups[1])
    grad_0 = synthesise(coef_0, power_0, groups[0])
    partial_1, grad_0 = lax.optimization_barrier((partial_1, grad_0))
    power_1 = sum_orders(partial_1)
    high_2 = exchange(high_2)
    grad_1 = synthesise(coef_1, power_1, groups[1])
    grad_0, grad_1 = lax.optimization_barrier((grad_0, grad_1))
    lat_0 = exchange(grad_0)
    spec_2 = jnp.concatenate([low_2, high_2], axis=1)
    coef_2, partial_2 = analyse(legendre_wide(spec_2, full_table), groups[2])
    power_2 = sum_orders(partial_2)
    lat_1 = exchange(grad_1)
    grad_2 = synthesise(coef_2, power_2, groups[2])
    lat_2 = exchange(grad_2)
    results = [
        to_grid(lat_0, groups[0]),
        to_grid(lat_1, groups[1]),
        to_grid(lat_2, groups[2]),
    ]
    return jnp.concatenate(results, axis=0)[None]


def solution(mesh):
    blocks = mesh.shape["mp"]

    def run(*arrays):
        return local(blocks, *arrays)

    return jax.shard_map(
        run,
        mesh=mesh,
        in_specs=(
            P("dp", None, "mp", None),
            P("dp", None, "mp", None),
            P("mp"),
            P("mp", "dp", None),
            P(),
            P(),
        ),
        out_specs=P("dp", None, "mp", None),
        check_vma=False,
    )
```
